256 devices in a mesh: azi: 8 (over y, core), rad: 16 (over x, z_lo), axl: 2 (over z_hi).
Axes of the slice: x: 4, y: 4, z: 8 (z_hi: 2, z_lo: 4; z = z_hi * 4 + z_lo), core: 2. Of those that a mesh axis runs over, the one named last changes fastest.
Arguments:
- perturbation: float32 [5, 8, 1024, 2048], P(None, 'axl', 'rad', 'azi'), may hold values from -6 to 6
- axial_velocity: float32 [8, 1024], P('axl', 'rad'), may hold values from 0.4 to 1.2
- swirl_velocity: float32 [8, 1024], P('axl', 'rad'), may hold values from -0.8 to 0.8
- sound_speed: float32 [8, 1024], P('axl', 'rad'), may hold values from 1 to 1.6
- rotor_offset: int32 [1], replicated, may hold values from 0 to 2047
Outputs:
- tendency: float32 [5, 8, 1024, 2048], P(None, 'axl', 'rad', 'azi')
The draws below stay inside these ranges and needn't reach their ends.
All inputs are finite; a program needn't handle non-finite values.
Results may differ from the reference program's by a relative error of at most 0.000065.
Values sent between devices are 32-bit elements; how exact they have to be, the bound alone decides.
No kernel may reach another device: no remote copies, remote signals or barrier semaphores. Data moves between devices by JAX's collectives and lax.ppermute only.
A program may use at most 128 MiB of HBM per device.

```python
import jax
import jax.numpy as jnp
import numpy as np
from jax import lax

NA = 2048
BAND = 128
NX = 8
NR = 1024


def block_scale(own_key, shape, pieces, smallest, high):
    factor_of, own = 1.0, jax.random.fold_in(own_key, 6)
    for axis_at, blocks in pieces:
        steps = jnp.exp(jax.random.uniform(jax.random.fold_in(own, axis_at), (blocks,), jnp.float32, smallest / len(pieces), high / len(pieces)))
        factor_of = factor_of * jnp.repeat(steps, shape[axis_at] // blocks).reshape([-1 if axis == axis_at else 1 for axis in range(len(shape))])
    return factor_of


def bell_draw(stream_key, shape, scale, most, cuts=(), kind=jnp.bfloat16):
    gain = block_scale(stream_key, shape, cuts, -0.22, 0.18) if cuts else 1.0
    entries = jax.random.normal(stream_key, shape, jnp.float32) * scale * gain
    return jnp.minimum(jnp.maximum(entries, -most), most).astype(kind)


def setup_inputs(seed: int = 0) -> dict:
    splits = jax.random.split(jax.random.key(seed), 6)
    perturbation = bell_draw(splits[0], (5, NX, NR, NA), 1.0, 6.0, ((1, 2), (2, 16), (3, 8)), jnp.float32)
    axial_velocity = jnp.clip(0.4 + 0.800000042 * jax.random.uniform(splits[1], (NX, NR), jnp.float32) ** block_scale(splits[1], (NX, NR), ((0, 2), (1, 16)), -0.2, 0.2), 0.4, 1.2)
    swirl_velocity = jnp.clip(jax.random.uniform(splits[2], (NX, NR), jnp.float32, -0.8, 0.8) * block_scale(splits[2], (NX, NR), ((0, 2), (1, 16)), -0.4, 0.0), -0.8, 0.8)
    sound_speed = jnp.clip(1.0 + 0.6 * jax.random.uniform(splits[3], (NX, NR), jnp.float32) ** block_scale(splits[3], (NX, NR), ((0, 2), (1, 16)), -0.2, 0.2), 1.0, 1.6)
    rotor_offset = jax.random.randint(splits[4], (1,), 0, NA).astype(jnp.int32)
    return {"perturbation": perturbation, "axial_velocity": axial_velocity, "swirl_velocity": swirl_velocity, "sound_speed": sound_speed, "rotor_offset": rotor_offset}


WEIGHTS = (45.0 / 60.0, -9.0 / 60.0, 1.0 / 60.0)


def stencil_coefs(cells, reach):
    offsets = np.arange(1, reach + 1)
    signs = np.where(offsets % 2 == 1, 1.0, -1.0)
    angles = np.pi * offsets / cells
    values = (np.pi / cells) * signs * np.cos(angles) / np.sin(angles)
    return np.concatenate([np.zeros(1), values])


def central_diff(padded, axis_pos):
    extent = padded.shape[axis_pos] - 6
    result = jnp.zeros_like(lax.slice_in_dim(padded, 3, 3 + extent, axis=axis_pos))
    for reach_k, weight in enumerate(WEIGHTS, start=1):
        upper = lax.slice_in_dim(padded, 3 + reach_k, 3 + reach_k + extent, axis=axis_pos)
        lower = lax.slice_in_dim(padded, 3 - reach_k, 3 - reach_k + extent, axis=axis_pos)
        result = result + weight * (upper - lower)
    return result


def section_terms(values, padded, angular, axial_vel, swirl_vel, sound_vel, metric):
    deriv_x = central_diff(padded, 1)
    stream = axial_vel[:, :, None]
    turning = (swirl_vel * metric[None, :])[:, :, None]
    speed_sq = (sound_vel * sound_vel)[:, :, None]
    scale = metric[:, None]
    convect = stream * deriv_x + turning * angular
    spread = deriv_x[1] + scale * angular[3]
    return jnp.stack([
        -(convect[0] + spread),
        -(convect[1] + deriv_x[4]),
        -convect[2],
        -(convect[3] + scale * angular[4]),
        -(convect[4] + speed_sq * spread),
    ])


def radial_terms(radial, sound_vel):
    speed_sq = (sound_vel * sound_vel)[:, :, None]
    blank = jnp.zeros_like(radial[0])
    return jnp.stack([-radial[0], blank, -radial[1], blank, -speed_sq * radial[0]])


def reference(perturbation, axial_velocity, swirl_velocity, sound_speed, rotor_offset):
    coefs = stencil_coefs(NA, BAND)
    waves = np.arange(NA // 2 + 1)
    phase = 2.0 * np.pi * (np.outer(waves, np.arange(1, BAND + 1)) % NA) / NA
    symbol_np = 2.0 * (np.sin(phase) * coefs[None, 1:]).sum(axis=1)
    symbol = jnp.asarray(symbol_np, dtype=jnp.float32)

    def one_field(field_in):
        spectrum = jnp.fft.rfft(field_in, axis=-1)
        return jnp.fft.irfft(spectrum * (1j * symbol), n=NA, axis=-1).astype(field_in.dtype)

    angular = lax.map(one_field, perturbation)
    shift_cells = rotor_offset[0]
    half = NX // 2
    stator = perturbation[:, :half]
    rotor = perturbation[:, half:]
    blanks = jnp.zeros_like(perturbation[:, :3])
    pad_stator = jnp.concatenate([blanks, stator, jnp.roll(rotor[:, :3], shift_cells, axis=-1)], axis=1)
    pad_rotor = jnp.concatenate([jnp.roll(stator[:, -3:], -shift_cells, axis=-1), rotor, blanks], axis=1)
    index = jnp.arange(NR).astype(perturbation.dtype)
    metric = 2.0 / (1.0 + (index + 0.5) / NR)
    first = section_terms(stator, pad_stator, angular[:, :half], axial_velocity[:half], swirl_velocity[:half], sound_speed[:half], metric)
    second = section_terms(rotor, pad_rotor, angular[:, half:], axial_velocity[half:], swirl_velocity[half:], sound_speed[half:], metric)
    partial_value = jnp.concatenate([first, second], axis=1)
    pair = jnp.stack([perturbation[2], perturbation[4]])
    pair_pad = jnp.pad(pair, ((0, 0), (0, 0), (3, 3), (0, 0)))
    radial = central_diff(pair_pad, 2)
    return partial_value + radial_terms(radial, sound_speed)
```

```python
import functools

import jax
import jax.numpy as jnp
import numpy as np
from jax import lax
from jax.experimental import pallas as pl
from jax.experimental.pallas import tpu as pltpu
from jax.sharding import PartitionSpec as P

NA = 2048
BAND = 128
WEIGHTS = (45.0 / 60.0, -9.0 / 60.0, 1.0 / 60.0)
AXES = ("azi", "rad", "axl")
TILE = 8
VMEM = pl.BlockSpec(memory_space=pltpu.VMEM)
SMEM = pl.BlockSpec(memory_space=pltpu.SMEM)


def stencil_coefs(cells, reach):
    offsets = np.arange(1, reach + 1)
    signs = np.where(offsets % 2 == 1, 1.0, -1.0)
    angles = np.pi * offsets / cells
    values = np.pi / cells * signs * np.cos(angles) / np.sin(angles)
    return np.concatenate([np.zeros(1), values])


def band_table(coefs, columns):
    reach = coefs.shape[0] - 1
    source = np.arange(columns + 2 * reach)
    target = np.arange(columns)
    offsets = source[:, None] - target[None, :] - reach
    magnitude = np.abs(offsets)
    picked = coefs[np.minimum(magnitude, reach)]
    return np.where(magnitude <= reach, np.sign(offsets) * picked, 0.0)


def neighbours(axis, step, wrap):
    count = lax.axis_size(axis)
    pairs = [(i, i + step) for i in range(count)]
    if wrap:
        return [(i, j % count) for i, j in pairs]
    return [(i, j) for i, j in pairs if 0 <= j < count]


def facing_pairs(blocks):
    azi_count, rad_count = lax.axis_size("azi"), lax.axis_size("rad")

    def place(azi, rad, axl):
        return (azi % azi_count * rad_count + rad) * 2 + axl

    pairs = []
    for azi in range(azi_count):
        for rad in range(rad_count):
            pairs.append((place(azi, rad, 0), place(azi - blocks, rad, 1)))
            pairs.append((place(azi, rad, 1), place(azi + blocks, rad, 0)))
    return pairs


def rotate_kernel(place_ref, own_ref, left_ref, right_ref, out_ref):
    start, side = place_ref[0], place_ref[1]
    fields, _, rows, cells = out_ref.shape
    tile, turn = start // BAND, start % BAND
    back = (BAND - turn) % BAND

    def fill(pieces):
        def body(step, carry):
            field, near = step // 3, step % 3
            plane = jnp.where(side == 0, 3 - near, near)
            lane = lax.broadcasted_iota(jnp.int32, (rows, BAND), 1)
            turned = [pltpu.roll(piece(field, plane), back, 1) for piece in pieces]
            keep = lane < BAND - turn
            out_ref[field, near, :, :BAND] = jnp.where(keep, turned[0], turned[1])
            out_ref[field, near, :, BAND:] = jnp.where(keep, turned[1], turned[2])
            return carry

        lax.fori_loop(0, fields * 3, body, 0)

    left = lambda f, p: left_ref[f, p]
    first = lambda f, p: own_ref[f, p, :, :BAND]
    second = lambda f, p: own_ref[f, p, :, BAND:]
    right = lambda f, p: right_ref[f, p]
    pl.when(tile == 0)(lambda: fill([left, first, second]))
    pl.when(tile == 1)(lambda: fill([first, second, right]))
    pl.when(tile == 2)(lambda: fill([second, right, right]))


def local_kernel(own_ref, left_ref, right_ref, low_ref, high_ref, scale_ref, band_ref, out_ref):
    fields, planes, rows, cells = own_ref.shape
    for plane in range(planes):
        def wide(kind):
            half = scale_ref[kind, plane]
            return jnp.concatenate([half, half], axis=1)

        stream, turning, speed_sq, metric = (wide(kind) for kind in range(4))

        def angular(field):
            line = jnp.concatenate(
                [left_ref[field, plane], own_ref[field, plane], right_ref[field, plane]], axis=1
            )
            return jnp.dot(
                line,
                band_ref[...],
                precision=lax.Precision.HIGHEST,
                preferred_element_type=jnp.float32,
            )

        def axial(field):
            total = jnp.zeros((rows, cells), jnp.float32)
            for reach, weight in enumerate(WEIGHTS, start=1):
                if plane + reach < planes:
                    total = total + weight * own_ref[field, plane + reach]
                if plane - reach >= 0:
                    total = total - weight * own_ref[field, plane - reach]
            return total

        def radial(which, field):
            lines = jnp.concatenate(
                [low_ref[which, plane], own_ref[field, plane], high_ref[which, plane]], axis=0
            )
            total = jnp.zeros((rows, cells), jnp.float32)
            for reach, weight in enumerate(WEIGHTS, start=1):
                upper = lines[TILE + reach : TILE + reach + rows]
                lower = lines[TILE - reach : TILE - reach + rows]
                total = total + weight * (upper - lower)
            return total

        deriv_1, deriv_4 = axial(1), axial(4)
        around_3 = angular(3)
        spread = deriv_1 + metric * around_3 + radial(0, 2)
        out_ref[0, plane] = -(stream * axial(0) + turning * angular(0) + spread)
        out_ref[1, plane] = -(stream * deriv_1 + turning * angular(1) + deriv_4)
        out_ref[2, plane] = -(stream * axial(2) + turning * angular(2) + radial(1, 4))
        around_4 = angular(4)
        out_ref[3, plane] = -(stream * axial(3) + turning * around_3 + metric * around_4)
        out_ref[4, plane] = -(stream * deriv_4 + turning * around_4 + speed_sq * spread)


def facing_kernel(place_ref, part_ref, facing_ref, scale_ref, out_ref):
    side = place_ref[1]
    sign = jnp.where(side == 0, 1.0, -1.0).astype(jnp.float32)
    fields, planes, rows, cells = part_ref.shape
    far = jnp.where(side == 0, 0, planes - 1)
    for field in range(fields):
        out_ref[field, far] = part_ref[field, far]

    def body(step, carry):
        lines = pl.ds(pl.multiple_of(step * TILE, TILE), TILE)
        for near in range(3):
            plane = jnp.where(side == 0, planes - 1 - near, near)

            def wide(kind):
                half = scale_ref[kind, plane, lines]
                return jnp.concatenate([half, half], axis=1)

            def deriv(field):
                total = (sign * WEIGHTS[near]) * facing_ref[field, 0, lines]
                for other in range(1, 3 - near):
                    total = total + (sign * WEIGHTS[near + other]) * facing_ref[field, other, lines]
                return total

            stream, speed_sq = wide(0), wide(2)
            derivs = [deriv(field) for field in range(fields)]
            extra = [derivs[1], derivs[4], None, None, speed_sq * derivs[1]]
            for field in range(fields):
                change = stream * derivs[field]
                if extra[field] is not None:
                    change = change + extra[field]
                out_ref[field, plane, lines] = part_ref[field, plane, lines] - change
        return carry

    lax.fori_loop(0, rows // TILE, body, 0)


def per_device(perturbation, axial_velocity, swirl_velocity, sound_speed, rotor_offset):
    fields, planes, rows, cells = perturbation.shape
    azi_count, rad_count = lax.axis_size("azi"), lax.axis_size("rad")
    side = lax.axis_index("axl")
    moved = rotor_offset[0] + BAND
    blocks = moved // cells % azi_count
    start = moved % cells
    place = jnp.stack([jnp.where(side == 0, start, cells - start), side]).astype(jnp.int32)

    left = lax.ppermute(perturbation[..., cells - BAND :], "azi", neighbours("azi", 1, True))
    right = lax.ppermute(perturbation[..., :BAND], "azi", neighbours("azi", -1, True))
    pair = jnp.stack([perturbation[2], perturbation[4]])
    low = lax.ppermute(pair[:, :, rows - TILE :], "rad", neighbours("rad", 1, False))
    high = lax.ppermute(pair[:, :, :TILE], "rad", neighbours("rad", -1, False))

    index = (lax.axis_index("rad") * rows + jnp.arange(rows, dtype=jnp.int32)).astype(jnp.float32)
    metric = 2.0 / (1.0 + (index + 0.5) / (rows * rad_count))
    scales = jnp.stack(
        [
            axial_velocity,
            swirl_velocity * metric,
            sound_speed * sound_speed,
            jnp.broadcast_to(metric, axial_velocity.shape),
        ]
    )
    scales = jnp.broadcast_to(scales[..., None], scales.shape + (BAND,))
    band = jnp.asarray(band_table(stencil_coefs(NA, BAND), cells), dtype=jnp.float32)

    sent = pl.pallas_call(
        rotate_kernel,
        out_shape=jax.ShapeDtypeStruct((fields, 3, rows, cells), jnp.float32),
        in_specs=[SMEM, VMEM, VMEM, VMEM],
        out_specs=VMEM,
        name="rotate",
    )(place, perturbation, left, right)

    def branch(shift):
        def run(place, perturbation, left, right, low, high, scales, sent):
            facing = lax.ppermute(sent, AXES, facing_pairs(shift))
            part = pl.pallas_call(
                local_kernel,
                out_shape=jax.ShapeDtypeStruct(perturbation.shape, jnp.float32),
                in_specs=[VMEM] * 7,
                out_specs=VMEM,
                name="local",
            )(perturbation, left, right, low, high, scales, band)
            return pl.pallas_call(
                facing_kernel,
                out_shape=jax.ShapeDtypeStruct(perturbation.shape, jnp.float32),
                in_specs=[SMEM, VMEM, VMEM, VMEM],
                out_specs=VMEM,
                name="facing",
            )(place, part, facing, scales)

        return run

    return lax.switch(
        blocks,
        [branch(shift) for shift in range(azi_count)],
        place, perturbation, left, right, low, high, scales, sent,
    )


def solution(mesh):
    return jax.shard_map(
        per_device,
        mesh=mesh,
        in_specs=(
            P(None, "axl", "rad", "azi"),
            P("axl", "rad"),
            P("axl", "rad"),
            P("axl", "rad"),
            P(),
        ),
        out_specs=P(None, "axl", "rad", "azi"),
        check_vma=False,
    )
```

```python
import jax
import jax.numpy as jnp
import ml_dtypes
import numpy as np
from jax import lax
from jax.experimental import pallas as pl
from jax.experimental.pallas import tpu as pltpu
from jax.sharding import PartitionSpec as P

NA = 2048
BAND = 128
WEIGHTS = (45.0 / 60.0, -9.0 / 60.0, 1.0 / 60.0)
AXES = ("azi", "rad", "axl")
TILE = 8
VMEM = pl.BlockSpec(memory_space=pltpu.VMEM)
SMEM = pl.BlockSpec(memory_space=pltpu.SMEM)


def stencil_coefs(cells, reach):
    offsets = np.arange(1, reach + 1)
    signs = np.where(offsets % 2 == 1, 1.0, -1.0)
    angles = np.pi * offsets / cells
    values = np.pi / cells * signs * np.cos(angles) / np.sin(angles)
    return np.concatenate([np.zeros(1), values])


def band_table(coefs, columns):
    reach = coefs.shape[0] - 1
    source = np.arange(columns + 2 * reach)
    target = np.arange(columns)
    offsets = source[:, None] - target[None, :] - reach
    magnitude = np.abs(offsets)
    picked = coefs[np.minimum(magnitude, reach)]
    return np.where(magnitude <= reach, np.sign(offsets) * picked, 0.0)


def neighbours(axis, step, wrap):
    count = lax.axis_size(axis)
    pairs = [(i, i + step) for i in range(count)]
    if wrap:
        return [(i, j % count) for i, j in pairs]
    return [(i, j) for i, j in pairs if 0 <= j < count]


def facing_pairs(blocks):
    azi_count, rad_count = lax.axis_size("azi"), lax.axis_size("rad")

    def place(azi, rad, axl):
        return (azi % azi_count * rad_count + rad) * 2 + axl

    pairs = []
    for azi in range(azi_count):
        for rad in range(rad_count):
            pairs.append((place(azi, rad, 0), place(azi - blocks, rad, 1)))
            pairs.append((place(azi, rad, 1), place(azi + blocks, rad, 0)))
    return pairs


def edges_kernel(own_ref, first_ref, second_ref, top_ref, bottom_ref, sems):
    rows = own_ref.shape[2]
    pairs = [
        (own_ref.at[:, :, :, pl.ds(0, BAND)], first_ref),
        (own_ref.at[:, :, :, pl.ds(BAND, BAND)], second_ref),
    ]
    for which, field in enumerate((2, 4)):
        pairs.append((own_ref.at[field, :, pl.ds(0, TILE)], top_ref.at[which]))
        pairs.append((own_ref.at[field, :, pl.ds(rows - TILE, TILE)], bottom_ref.at[which]))
    copies = [pltpu.make_async_copy(a, b, sems.at[i]) for i, (a, b) in enumerate(pairs)]
    for copy in copies:
        copy.start()
    for copy in copies:
        copy.wait()


def rotate_kernel(place_ref, own_ref, left_ref, right_ref, out_ref):
    start, side = place_ref[0], place_ref[1]
    fields, _, rows, cells = out_ref.shape
    tile, turn = start // BAND, start % BAND
    back = (BAND - turn) % BAND

    def fill(pieces):
        def body(field, carry):
            lane = lax.broadcasted_iota(jnp.int32, (rows, BAND), 1)
            keep = lane < BAND - turn
            for near in range(3):
                plane = jnp.where(side == 0, 3 - near, near)
                turned = [pltpu.roll(piece(field, plane), back, 1) for piece in pieces]
                out_ref[field, near, :, :BAND] = jnp.where(keep, turned[0], turned[1])
                out_ref[field, near, :, BAND:] = jnp.where(keep, turned[1], turned[2])
            return carry

        lax.fori_loop(0, fields, body, 0)

    left = lambda f, p: left_ref[f, p]
    first = lambda f, p: own_ref[f, p, :, :BAND]
    second = lambda f, p: own_ref[f, p, :, BAND:]
    right = lambda f, p: right_ref[f, p]
    pl.when(tile == 0)(lambda: fill([left, first, second]))
    pl.when(tile == 1)(lambda: fill([first, second, right]))
    pl.when(tile == 2)(lambda: fill([second, right, right]))


def local_kernel(
    mix_ref, own_ref, left_ref, right_ref, low_ref, high_ref, scale_ref, band_ref, out_ref, tall_ref
):
    fields, planes, rows, cells = own_ref.shape
    chunk = 2 * TILE

    def fill(step, carry):
        which, plane = step // planes, step % planes
        tall_ref[which, plane, :TILE] = low_ref[which, plane]
        tall_ref[which, plane, TILE : TILE + rows] = own_ref[2 + 2 * which, plane]
        tall_ref[which, plane, TILE + rows :] = high_ref[which, plane]
        return carry

    lax.fori_loop(0, 2 * planes, fill, 0)

    def body(step, carry):
        plane, place = step % planes, step // planes
        first = pl.multiple_of(place * chunk, chunk)
        lines = pl.ds(first, chunk)

        def wide(kind):
            half = scale_ref[kind, plane, lines]
            return jnp.concatenate([half, half], axis=1)

        window = jnp.concatenate(
            [
                jnp.concatenate(
                    [
                        left_ref[field, plane, lines],
                        own_ref[field, plane, lines],
                        right_ref[field, plane, lines],
                    ],
                    axis=1,
                )
                for field in range(fields)
            ],
            axis=0,
        )
        coarse = window.astype(jnp.bfloat16)
        fine = (window - coarse.astype(jnp.float32)).astype(jnp.bfloat16)

        def product(values, part):
            return jnp.dot(values, band_ref[part], preferred_element_type=jnp.float32)

        turned = product(fine, 0) + product(coarse, 1) + product(coarse, 0)
        angular = [turned[field * chunk : (field + 1) * chunk] for field in range(fields)]

        def axial(field):
            total = mix_ref[plane * planes] * own_ref[field, 0, lines]
            for other in range(1, planes):
                total = total + mix_ref[plane * planes + other] * own_ref[field, other, lines]
            return total

        def radial(which):
            tall = tall_ref[which, plane, pl.ds(first, chunk + 2 * TILE)]
            total = jnp.zeros((chunk, cells), jnp.float32)
            for reach, weight in enumerate(WEIGHTS, start=1):
                upper = tall[TILE + reach : TILE + reach + chunk]
                lower = tall[TILE - reach : TILE - reach + chunk]
                total = total + weight * (upper - lower)
            return total

        stream, turning, speed_sq, metric = (wide(kind) for kind in range(4))
        deriv_1, deriv_4 = axial(1), axial(4)
        spread = deriv_1 + metric * angular[3] + radial(0)
        out_ref[0, plane, lines] = -(stream * axial(0) + turning * angular[0] + spread)
        out_ref[1, plane, lines] = -(stream * deriv_1 + turning * angular[1] + deriv_4)
        out_ref[2, plane, lines] = -(stream * axial(2) + turning * angular[2] + radial(1))
        out_ref[3, plane, lines] = -(
            stream * axial(3) + turning * angular[3] + metric * angular[4]
        )
        out_ref[4, plane, lines] = -(
            stream * deriv_4 + turning * angular[4] + speed_sq * spread
        )
        return carry

    lax.fori_loop(0, planes * (rows // chunk), body, 0)


def facing_kernel(place_ref, part_ref, facing_ref, scale_ref, out_ref):
    side = place_ref[1]
    sign = jnp.where(side == 0, 1.0, -1.0).astype(jnp.float32)
    fields, planes, rows, cells = part_ref.shape
    far = jnp.where(side == 0, 0, planes - 1)

    def body(step, carry):
        lines = pl.ds(pl.multiple_of(step * TILE, TILE), TILE)
        for field in range(fields):
            out_ref[field, far, lines] = part_ref[field, far, lines]
        for near in range(3):
            plane = jnp.where(side == 0, planes - 1 - near, near)

            def wide(kind):
                half = scale_ref[kind, plane, lines]
                return jnp.concatenate([half, half], axis=1)

            def deriv(field):
                total = (sign * WEIGHTS[near]) * facing_ref[field, 0, lines]
                for other in range(1, 3 - near):
                    total = total + (sign * WEIGHTS[near + other]) * facing_ref[field, other, lines]
                return total

            stream, speed_sq = wide(0), wide(2)
            derivs = [deriv(field) for field in range(fields)]
            extra = [derivs[1], derivs[4], None, None, speed_sq * derivs[1]]
            for field in range(fields):
                change = stream * derivs[field]
                if extra[field] is not None:
                    change = change + extra[field]
                out_ref[field, plane, lines] = part_ref[field, plane, lines] - change
        return carry

    lax.fori_loop(0, rows // TILE, body, 0)


def per_device(perturbation, axial_velocity, swirl_velocity, sound_speed, rotor_offset):
    fields, planes, rows, cells = perturbation.shape
    azi_count, rad_count = lax.axis_size("azi"), lax.axis_size("rad")
    side = lax.axis_index("axl")
    moved = rotor_offset[0] + BAND
    blocks = moved // cells % azi_count
    start = moved % cells
    place = jnp.stack([jnp.where(side == 0, start, cells - start), side]).astype(jnp.int32)

    half = jax.ShapeDtypeStruct((fields, planes, rows, BAND), jnp.float32)
    edge = jax.ShapeDtypeStruct((2, planes, TILE, cells), jnp.float32)
    first, second, top, bottom = pl.pallas_call(
        edges_kernel,
        out_shape=(half, half, edge, edge),
        in_specs=[pl.BlockSpec(memory_space=pl.ANY)],
        out_specs=(VMEM,) * 4,
        scratch_shapes=[pltpu.SemaphoreType.DMA((6,))],
        name="edges",
    )(perturbation)
    left = lax.ppermute(second, "azi", neighbours("azi", 1, True))
    right = lax.ppermute(first, "azi", neighbours("azi", -1, True))
    low = lax.ppermute(bottom, "rad", neighbours("rad", 1, False))
    high = lax.ppermute(top, "rad", neighbours("rad", -1, False))

    index = (lax.axis_index("rad") * rows + jnp.arange(rows, dtype=jnp.int32)).astype(jnp.float32)
    metric = 2.0 / (1.0 + (index + 0.5) / (rows * rad_count))
    scales = jnp.stack(
        [
            axial_velocity,
            swirl_velocity * metric,
            sound_speed * sound_speed,
            jnp.broadcast_to(metric, axial_velocity.shape),
        ]
    )
    scales = jnp.broadcast_to(scales[..., None], scales.shape + (BAND,))
    table = band_table(stencil_coefs(NA, BAND), cells).astype(np.float32)
    coarse = table.astype(ml_dtypes.bfloat16)
    fine = (table - coarse.astype(np.float32)).astype(ml_dtypes.bfloat16)
    band = jnp.asarray(np.stack([coarse, fine]))
    mix = np.zeros((planes, planes))
    for reach, weight in enumerate(WEIGHTS, start=1):
        mix += weight * (np.eye(planes, k=reach) - np.eye(planes, k=-reach))
    mix = jnp.asarray(mix.reshape(-1), dtype=jnp.float32)

    sent = pl.pallas_call(
        rotate_kernel,
        out_shape=jax.ShapeDtypeStruct((fields, 3, rows, cells), jnp.float32),
        in_specs=[SMEM, VMEM, VMEM, VMEM],
        out_specs=VMEM,
        name="rotate",
    )(place, perturbation, left, right)

    def branch(shift):
        def run(sent, *terms):
            facing = lax.ppermute(sent, AXES, facing_pairs(shift))
            part = pl.pallas_call(
                local_kernel,
                out_shape=jax.ShapeDtypeStruct(perturbation.shape, jnp.float32),
                in_specs=[SMEM] + [VMEM] * 7,
                out_specs=VMEM,
                scratch_shapes=[pltpu.VMEM((2, planes, rows + 2 * TILE, cells), jnp.float32)],
                name="local",
            )(*terms)
            return facing, part

        return run

    facing, part = lax.switch(
        blocks,
        [branch(shift) for shift in range(azi_count)],
        sent, mix, perturbation, left, right, low, high, scales, band,
    )
    step = 2 * TILE

    def by_rows(shape):
        return pl.BlockSpec((shape[0], shape[1], step, shape[3]), lambda i: (0, 0, i, 0))

    return pl.pallas_call(
        facing_kernel,
        out_shape=jax.ShapeDtypeStruct(perturbation.shape, jnp.float32),
        grid=(rows // step,),
        in_specs=[SMEM] + [by_rows(v.shape) for v in (part, facing, scales)],
        out_specs=by_rows(perturbation.shape),
        name="facing",
    )(place, part, facing, scales)


def solution(mesh):
    return jax.shard_map(
        per_device,
        mesh=mesh,
        in_specs=(
            P(None, "axl", "rad", "azi"),
            P("axl", "rad"),
            P("axl", "rad"),
            P("axl", "rad"),
            P(),
        ),
        out_specs=P(None, "axl", "rad", "azi"),
        check_vma=False,
    )
```

```python
import jax
import jax.numpy as jnp
import ml_dtypes
import numpy as np
from jax import lax
from jax.experimental import pallas as pl
from jax.experimental.pallas import tpu as pltpu
from jax.sharding import PartitionSpec as P

NA = 2048
BAND = 128
WEIGHTS = (45.0 / 60.0, -9.0 / 60.0, 1.0 / 60.0)
AXES = ("azi", "rad", "axl")
TILE = 8
VMEM = pl.BlockSpec(memory_space=pltpu.VMEM)
SMEM = pl.BlockSpec(memory_space=pltpu.SMEM)
ANY = pl.BlockSpec(memory_space=pl.ANY)
HBM = pl.BlockSpec(memory_space=pltpu.HBM)
REACH = 3
ROWS_A = 32
FREE = pl.CostEstimate(flops=0, bytes_accessed=0, transcendentals=0)
PARAMS = pltpu.CompilerParams(vmem_limit_bytes=12 * 2**20)


def stencil_coefs(cells, reach):
    offsets = np.arange(1, reach + 1)
    signs = np.where(offsets % 2 == 1, 1.0, -1.0)
    angles = np.pi * offsets / cells
    values = np.pi / cells * signs * np.cos(angles) / np.sin(angles)
    return np.concatenate([np.zeros(1), values])


def band_table(coefs, columns):
    reach = coefs.shape[0] - 1
    source = np.arange(columns + 2 * reach)
    target = np.arange(columns)
    offsets = source[:, None] - target[None, :] - reach
    magnitude = np.abs(offsets)
    picked = coefs[np.minimum(magnitude, reach)]
    return np.where(magnitude <= reach, np.sign(offsets) * picked, 0.0)


def neighbours(axis, step, wrap):
    count = lax.axis_size(axis)
    pairs = [(i, (i + step) % count) for i in range(count)]
    return pairs if wrap else [(i, j) for i, j in pairs if abs(i - j) == 1]


def facing_pairs(blocks):
    azi_count, rad_count = lax.axis_size("azi"), lax.axis_size("rad")

    def place(azi, rad, axl):
        return (azi % azi_count * rad_count + rad) * 2 + axl

    pairs = []
    for azi in range(azi_count):
        for rad in range(rad_count):
            pairs.append((place(azi, rad, 0), place(azi - blocks, rad, 1)))
            pairs.append((place(azi, rad, 1), place(azi + blocks, rad, 0)))
    return pairs


def near_plane(near, planes):
    return jnp.where(lax.axis_index("axl") == 0, planes - 1 - near, near)


def run_copies(pairs, sems):
    copies = [pltpu.make_async_copy(a, b, sems.at[i]) for i, (a, b) in enumerate(pairs)]
    for copy in copies:
        copy.start()
    for copy in copies:
        copy.wait()


def facing_edge_kernel(own_ref, out_ref, sems):
    planes, rows = own_ref.shape[1], out_ref.shape[2]
    run_copies(
        [
            (own_ref.at[:, near_plane(near, planes), pl.ds(0, rows)], out_ref.at[:, near])
            for near in range(3)
        ],
        sems,
    )


def edges_kernel(own_ref, _, first_ref, second_ref, top_ref, bottom_ref, sems):
    planes, rows = own_ref.shape[1:3]
    pairs = [
        (own_ref.at[:, :, :, pl.ds(0, BAND)], first_ref),
        (own_ref.at[:, :, :, pl.ds(BAND, BAND)], second_ref),
    ]
    copies = [pltpu.make_async_copy(a, b, sems.at[i]) for i, (a, b) in enumerate(pairs)]
    for copy in copies:
        copy.start()

    def line_of(line, carry):
        field, plane = 2 + 2 * (line // planes), line % planes
        head = own_ref[field, plane, :TILE]
        tail = own_ref[field, plane, rows - TILE :]
        for step in range(REACH):
            top_ref[step, pl.ds(line, 1)] = head[step : step + 1]
            bottom_ref[step, pl.ds(line, 1)] = tail[TILE - REACH + step : TILE - REACH + step + 1]
        return carry

    lax.fori_loop(0, 2 * planes, line_of, 0)
    for copy in copies:
        copy.wait()


def split_kernel(own_ref, first_ref, second_ref, sems):
    run_copies(
        [
            (own_ref.at[:, :, :, pl.ds(0, BAND)], first_ref),
            (own_ref.at[:, :, :, pl.ds(BAND, BAND)], second_ref),
        ],
        sems,
    )


def rotate_kernel(before, first_row, offset_ref, own_ref, left_ref, right_ref, out_ref):
    fields, _, rows, cells = out_ref.shape
    moved = (offset_ref[0] + BAND) % cells
    forward = lax.axis_index("axl") == (0 if before else 1)
    start = jnp.where(forward, moved, cells - moved)
    tile, turn = start // BAND, start % BAND
    back = (BAND - turn) % BAND
    lines = pl.ds(first_row, rows)

    def body(field, carry):
        keep = lax.broadcasted_iota(jnp.int32, (rows, BAND), 1) < BAND - turn
        for near in range(3):
            plane = near_plane(near, own_ref.shape[1]) if before else near
            tiles = [
                left_ref[field, plane, lines],
                own_ref[field, plane, lines, :BAND],
                own_ref[field, plane, lines, BAND:],
                right_ref[field, plane, lines],
            ]
            tiles.append(tiles[-1])
            turned = [
                pltpu.roll(
                    jnp.where(tile == 0, tiles[i], jnp.where(tile == 1, tiles[i + 1], tiles[i + 2])),
                    back,
                    1,
                )
                for i in range(3)
            ]
            out_ref[field, near, :, :BAND] = jnp.where(keep, turned[0], turned[1])
            out_ref[field, near, :, BAND:] = jnp.where(keep, turned[1], turned[2])
        return carry

    lax.fori_loop(0, fields, body, 0)


def local_kernel(
    mix_ref, own_ref, left_ref, right_ref, low_ref, high_ref, scale_ref, band_ref, out_ref, tall_ref
):
    fields, planes, rows, cells = own_ref.shape
    chunk = 2 * TILE

    def fill(line, carry):
        which, plane = line // planes, line % planes
        tall_ref[which, plane, TILE : TILE + rows] = own_ref[2 + 2 * which, plane]
        for step in range(REACH):
            tall_ref[which, plane, TILE - REACH + step : TILE - REACH + step + 1] = low_ref[step, pl.ds(line, 1)]
            tall_ref[which, plane, TILE + rows + step : TILE + rows + step + 1] = high_ref[step, pl.ds(line, 1)]
        return carry

    lax.fori_loop(0, 2 * planes, fill, 0)

    def body(step, carry):
        plane, place = step % planes, step // planes
        first = pl.multiple_of(place * chunk, chunk)
        lines = pl.ds(first, chunk)

        def wide(kind):
            half = scale_ref[kind, plane, lines]
            return jnp.concatenate([half, half], axis=1)

        window = jnp.concatenate(
            [
                jnp.concatenate(
                    [
                        left_ref[field, plane, lines],
                        own_ref[field, plane, lines],
                        right_ref[field, plane, lines],
                    ],
                    axis=1,
                )
                for field in range(fields)
            ],
            axis=0,
        )
        coarse = window.astype(jnp.bfloat16)
        fine = (window - coarse.astype(jnp.float32)).astype(jnp.bfloat16)

        def product(values, part):
            return jnp.dot(values, band_ref[part], preferred_element_type=jnp.float32)

        turned = product(fine, 0) + product(coarse, 1) + product(coarse, 0)
        angular = [turned[field * chunk : (field + 1) * chunk] for field in range(fields)]

        def axial(field):
            total = mix_ref[plane * planes] * own_ref[field, 0, lines]
            for other in range(1, planes):
                total = total + mix_ref[plane * planes + other] * own_ref[field, other, lines]
            return total

        def radial(which):
            tall = tall_ref[which, plane, pl.ds(first, chunk + 2 * TILE)]
            total = jnp.zeros((chunk, cells), jnp.float32)
            for reach, weight in enumerate(WEIGHTS, start=1):
                upper = tall[TILE + reach : TILE + reach + chunk]
                lower = tall[TILE - reach : TILE - reach + chunk]
                total = total + weight * (upper - lower)
            return total

        stream, speed_sq, turning, metric = (wide(kind) for kind in range(4))
        deriv_1, deriv_4 = axial(1), axial(4)
        spread = deriv_1 + metric * angular[3] + radial(0)
        out_ref[0, plane, lines] = -(stream * axial(0) + turning * angular[0] + spread)
        out_ref[1, plane, lines] = -(stream * deriv_1 + turning * angular[1] + deriv_4)
        out_ref[2, plane, lines] = -(stream * axial(2) + turning * angular[2] + radial(1))
        out_ref[3, plane, lines] = -(
            stream * axial(3) + turning * angular[3] + metric * angular[4]
        )
        out_ref[4, plane, lines] = -(
            stream * deriv_4 + turning * angular[4] + speed_sq * spread
        )
        return carry

    lax.fori_loop(0, planes * (rows // chunk), body, 0)


def facing_kernel(first_row, part_ref, facing_ref, scale_ref, *refs):
    out_ref, stage_ref, sems = refs[-3:]
    side = lax.axis_index("axl")
    sign = jnp.where(side == 0, 1.0, -1.0).astype(jnp.float32)
    fields, planes, _, cells = part_ref.shape
    rows = facing_ref.shape[2]
    count = rows // TILE

    def copies(step):
        start = pl.multiple_of(step * TILE, TILE)
        return [
            pltpu.make_async_copy(
                stage_ref.at[:, near, pl.ds(start, TILE)],
                out_ref.at[:, near_plane(near, planes), pl.ds(first_row + start, TILE)],
                sems.at[REACH * step + near],
            )
            for near in range(REACH)
        ]

    if first_row == 0:
        far = near_plane(REACH, planes)
        spare = pltpu.make_async_copy(part_ref.at[:, far], out_ref.at[:, far], sems.at[REACH * count])
        spare.start()

    def body(step, carry):
        start = pl.multiple_of(step * TILE, TILE)
        lines, here = pl.ds(first_row + start, TILE), pl.ds(start, TILE)
        for near in range(REACH):
            plane = near_plane(near, planes)

            def wide(kind):
                half = scale_ref[kind, plane, lines]
                return jnp.concatenate([half, half], axis=1)

            def deriv(field):
                total = (sign * WEIGHTS[near]) * facing_ref[field, 0, here]
                for other in range(1, REACH - near):
                    total = total + (sign * WEIGHTS[near + other]) * facing_ref[field, other, here]
                return total

            stream, speed_sq = wide(0), wide(1)
            derivs = [deriv(field) for field in range(fields)]
            extra = [derivs[1], derivs[4], None, None, speed_sq * derivs[1]]
            for field in range(fields):
                change = stream * derivs[field]
                if extra[field] is not None:
                    change = change + extra[field]
                stage_ref[field, near, here] = part_ref[field, plane, lines] - change
        for copy in copies(step):
            copy.start()
        return carry

    def finish(step, carry):
        for copy in copies(step):
            copy.wait()
        return carry

    lax.fori_loop(0, count, body, 0)
    lax.fori_loop(0, count, finish, 0)
    if first_row == 0:
        spare.wait()


def per_device(perturbation, axial_velocity, swirl_velocity, sound_speed, rotor_offset):
    fields, planes, rows, cells = perturbation.shape
    azi_count, rad_count = lax.axis_size("azi"), lax.axis_size("rad")
    blocks = (rotor_offset[0] + BAND) // cells % azi_count

    index = (lax.axis_index("rad") * rows + jnp.arange(rows, dtype=jnp.int32)).astype(jnp.float32)
    metric = 2.0 / (1.0 + (index + 0.5) / (rows * rad_count))

    def spread_scales(axial_velocity, swirl_velocity, sound_speed):
        scales = jnp.stack(
            [
                axial_velocity,
                sound_speed * sound_speed,
                swirl_velocity * metric,
                jnp.broadcast_to(metric, axial_velocity.shape),
            ]
        )
        return jnp.broadcast_to(scales[..., None], scales.shape + (BAND,))

    table = band_table(stencil_coefs(NA, BAND), cells).astype(np.float32)
    coarse = table.astype(ml_dtypes.bfloat16)
    fine = (table - coarse.astype(np.float32)).astype(ml_dtypes.bfloat16)
    band = jnp.asarray(np.stack([coarse, fine]))
    mix = np.zeros((planes, planes))
    for reach, weight in enumerate(WEIGHTS, start=1):
        mix += weight * (np.eye(planes, k=reach) - np.eye(planes, k=-reach))
    mix = jnp.asarray(mix.reshape(-1), dtype=jnp.float32)

    rows_a = ROWS_A
    rows_b = rows - rows_a

    def array(*shape):
        return jax.ShapeDtypeStruct(shape, jnp.float32)

    def exchange(first, second):
        left = lax.ppermute(second, "azi", neighbours("azi", 1, True))
        right = lax.ppermute(first, "azi", neighbours("azi", -1, True))
        return left, right

    def rotate(before, first_row, count, *values):
        return pl.pallas_call(
            lambda *refs: rotate_kernel(before, first_row, *refs),
            out_shape=array(fields, 3, count, cells),
            in_specs=[SMEM, VMEM, VMEM, VMEM],
            out_specs=VMEM,
            compiler_params=PARAMS,
            cost_estimate=FREE,
            name="rotate",
        )(*values)

    def facing_step(first, part, facing, scales, *done):
        return pl.pallas_call(
            lambda *refs: facing_kernel(first, *refs),
            out_shape=array(*part.shape),
            in_specs=[VMEM] * 3 + [HBM] * len(done),
            out_specs=HBM,
            scratch_shapes=[
                pltpu.VMEM(facing.shape, jnp.float32),
                pltpu.SemaphoreType.DMA((REACH * (facing.shape[2] // TILE) + 1,)),
            ],
            input_output_aliases={3: 0} if done else {},
            compiler_params=PARAMS,
            cost_estimate=FREE,
            name="facing",
        )(part, facing, scales, *done)

    def branch(shift):
        pairs = facing_pairs(shift)

        def run(rotor_offset, mix, perturbation, band, *speeds):
            sent_a = pl.pallas_call(
                facing_edge_kernel,
                out_shape=array(fields, 3, rows_a, cells),
                in_specs=[ANY],
                out_specs=VMEM,
                scratch_shapes=[pltpu.SemaphoreType.DMA((3,))],
                compiler_params=PARAMS,
                cost_estimate=FREE,
                name="facing_edge",
            )(perturbation)
            first, second, top, bottom = pl.pallas_call(
                edges_kernel,
                out_shape=(array(fields, planes, rows, BAND),) * 2 + (array(REACH, 2 * planes, cells),) * 2,
                in_specs=[VMEM, ANY],
                out_specs=(VMEM,) * 4,
                scratch_shapes=[pltpu.SemaphoreType.DMA((2,))],
                compiler_params=PARAMS,
                cost_estimate=FREE,
                name="edges",
            )(perturbation, sent_a)
            left, right = exchange(first, second)
            low = lax.ppermute(bottom, "rad", neighbours("rad", 1, False))
            high = lax.ppermute(top, "rad", neighbours("rad", -1, False))
            facing_a = lax.ppermute(sent_a, AXES, pairs)
            left, right, speeds = lax.optimization_barrier((left, right, speeds))
            scales = spread_scales(*speeds)
            sent_b = rotate(True, rows_a, rows_b, rotor_offset, perturbation, left, right)
            sent_b, facing_a, low, high = lax.optimization_barrier((sent_b, facing_a, low, high))
            facing_b = lax.ppermute(sent_b, AXES, pairs)
            part = pl.pallas_call(
                local_kernel,
                out_shape=array(*perturbation.shape),
                in_specs=[SMEM] + [VMEM] * 7,
                out_specs=VMEM,
                scratch_shapes=[pltpu.VMEM((2, planes, rows + 2 * TILE, cells), jnp.float32)],
                compiler_params=PARAMS,
                cost_estimate=FREE,
                name="local",
            )(mix, perturbation, left, right, low, high, scales, band)
            halves = pl.pallas_call(
                split_kernel,
                out_shape=(array(fields, 3, rows_a, BAND),) * 2,
                in_specs=[ANY],
                out_specs=(VMEM,) * 2,
                scratch_shapes=[pltpu.SemaphoreType.DMA((2,))],
                compiler_params=PARAMS,
                cost_estimate=FREE,
                name="split",
            )(facing_a)
            turned_a = rotate(False, 0, rows_a, rotor_offset, facing_a, *exchange(*halves))
            done_a = facing_step(0, part, turned_a, scales)
            return facing_step(rows_a, part, facing_b, scales, done_a)

        return run

    mix, band = lax.optimization_barrier((mix, band))
    return lax.switch(
        blocks,
        [branch(shift) for shift in range(azi_count)],
        rotor_offset, mix, perturbation, band, axial_velocity, swirl_velocity, sound_speed,
    )


def solution(mesh):
    return jax.shard_map(
        per_device,
        mesh=mesh,
        in_specs=(
            P(None, "axl", "rad", "azi"),
            P("axl", "rad"),
            P("axl", "rad"),
            P("axl", "rad"),
            P(),
        ),
        out_specs=P(None, "axl", "rad", "azi"),
        check_vma=False,
    )
```

```python
import jax
import jax.numpy as jnp
import ml_dtypes
import numpy as np
from jax import lax
from jax.experimental import pallas as pl
from jax.experimental.pallas import tpu as pltpu
from jax.sharding import PartitionSpec as P

NA = 2048
BAND = 128
WEIGHTS = (45.0 / 60.0, -9.0 / 60.0, 1.0 / 60.0)
AXES = ("azi", "rad", "axl")
TILE = 8
VMEM = pl.BlockSpec(memory_space=pltpu.VMEM)
SMEM = pl.BlockSpec(memory_space=pltpu.SMEM)
ANY = pl.BlockSpec(memory_space=pl.ANY)
HBM = pl.BlockSpec(memory_space=pltpu.HBM)
REACH = 3
ROWS_A = 32
FREE = pl.CostEstimate(flops=0, bytes_accessed=0, transcendentals=0)
PARAMS = pltpu.CompilerParams(vmem_limit_bytes=12 * 2**20)


def stencil_coefs(cells, reach):
    offsets = np.arange(1, reach + 1)
    signs = np.where(offsets % 2 == 1, 1.0, -1.0)
    angles = np.pi * offsets / cells
    values = np.pi / cells * signs * np.cos(angles) / np.sin(angles)
    return np.concatenate([np.zeros(1), values])


def band_table(coefs, columns):
    reach = coefs.shape[0] - 1
    source = np.arange(columns + 2 * reach)
    target = np.arange(columns)
    offsets = source[:, None] - target[None, :] - reach
    magnitude = np.abs(offsets)
    picked = coefs[np.minimum(magnitude, reach)]
    return np.where(magnitude <= reach, np.sign(offsets) * picked, 0.0)


def neighbours(axis, step, wrap):
    count = lax.axis_size(axis)
    pairs = [(i, (i + step) % count) for i in range(count)]
    return pairs if wrap else [(i, j) for i, j in pairs if abs(i - j) == 1]


def facing_pairs(blocks):
    azi_count, rad_count = lax.axis_size("azi"), lax.axis_size("rad")

    def place(azi, rad, axl):
        return (azi % azi_count * rad_count + rad) * 2 + axl

    pairs = []
    for azi in range(azi_count):
        for rad in range(rad_count):
            pairs.append((place(azi, rad, 0), place(azi - blocks, rad, 1)))
            pairs.append((place(azi, rad, 1), place(azi + blocks, rad, 0)))
    return pairs


def near_plane(near, planes):
    return jnp.where(lax.axis_index("axl") == 0, planes - 1 - near, near)


def run_copies(pairs, sems):
    copies = [pltpu.make_async_copy(a, b, sems.at[i]) for i, (a, b) in enumerate(pairs)]
    for copy in copies:
        copy.start()
    for copy in copies:
        copy.wait()


def facing_edge_kernel(own_ref, out_ref, sems):
    planes, rows = own_ref.shape[1], out_ref.shape[2]
    run_copies(
        [
            (own_ref.at[:, near_plane(near, planes), pl.ds(0, rows)], out_ref.at[:, near])
            for near in range(3)
        ],
        sems,
    )


def edges_kernel(own_ref, _, first_ref, second_ref, top_ref, bottom_ref, sems):
    planes, rows = own_ref.shape[1:3]
    pairs = [
        (own_ref.at[:, :, :, pl.ds(0, BAND)], first_ref),
        (own_ref.at[:, :, :, pl.ds(BAND, BAND)], second_ref),
    ]
    copies = [pltpu.make_async_copy(a, b, sems.at[i]) for i, (a, b) in enumerate(pairs)]
    for copy in copies:
        copy.start()

    def line_of(line, carry):
        field, plane = 2 + 2 * (line // planes), line % planes
        head = own_ref[field, plane, :TILE]
        tail = own_ref[field, plane, rows - TILE :]
        for step in range(REACH):
            top_ref[step, pl.ds(line, 1)] = head[step : step + 1]
            bottom_ref[step, pl.ds(line, 1)] = tail[TILE - REACH + step : TILE - REACH + step + 1]
        return carry

    lax.fori_loop(0, 2 * planes, line_of, 0)
    for copy in copies:
        copy.wait()


def split_kernel(own_ref, first_ref, second_ref, sems):
    run_copies(
        [
            (own_ref.at[:, :, :, pl.ds(0, BAND)], first_ref),
            (own_ref.at[:, :, :, pl.ds(BAND, BAND)], second_ref),
        ],
        sems,
    )


def rotate_kernel(before, first_row, offset_ref, own_ref, left_ref, right_ref, out_ref):
    fields, _, rows, cells = out_ref.shape
    moved = (offset_ref[0] + BAND) % cells
    forward = lax.axis_index("axl") == (0 if before else 1)
    start = jnp.where(forward, moved, cells - moved)
    tile, turn = start // BAND, start % BAND
    back = (BAND - turn) % BAND
    lines = pl.ds(first_row, rows)

    def body(field, carry):
        keep = lax.broadcasted_iota(jnp.int32, (rows, BAND), 1) < BAND - turn
        for near in range(3):
            plane = near_plane(near, own_ref.shape[1]) if before else near
            tiles = [
                left_ref[field, plane, lines],
                own_ref[field, plane, lines, :BAND],
                own_ref[field, plane, lines, BAND:],
                right_ref[field, plane, lines],
            ]
            tiles.append(tiles[-1])
            turned = [
                pltpu.roll(
                    jnp.where(tile == 0, tiles[i], jnp.where(tile == 1, tiles[i + 1], tiles[i + 2])),
                    back,
                    1,
                )
                for i in range(3)
            ]
            out_ref[field, near, :, :BAND] = jnp.where(keep, turned[0], turned[1])
            out_ref[field, near, :, BAND:] = jnp.where(keep, turned[1], turned[2])
        return carry

    lax.fori_loop(0, fields, body, 0)


def local_kernel(
    mix_ref, own_ref, left_ref, right_ref, low_ref, high_ref, scale_ref, band_ref, out_ref, tall_ref
):
    fields, planes, rows, cells = own_ref.shape
    chunk = 2 * TILE

    def fill(line, carry):
        which, plane = line // planes, line % planes
        tall_ref[which, plane, TILE : TILE + rows] = own_ref[2 + 2 * which, plane]
        for step in range(REACH):
            tall_ref[which, plane, TILE - REACH + step : TILE - REACH + step + 1] = low_ref[step, pl.ds(line, 1)]
            tall_ref[which, plane, TILE + rows + step : TILE + rows + step + 1] = high_ref[step, pl.ds(line, 1)]
        return carry

    lax.fori_loop(0, 2 * planes, fill, 0)

    def body(step, carry):
        plane, place = step % planes, step // planes
        first = pl.multiple_of(place * chunk, chunk)
        lines = pl.ds(first, chunk)

        def wide(kind):
            half = scale_ref[kind, plane, lines]
            return jnp.concatenate([half, half], axis=1)

        window = jnp.concatenate(
            [
                jnp.concatenate(
                    [
                        left_ref[field, plane, lines],
                        own_ref[field, plane, lines],
                        right_ref[field, plane, lines],
                    ],
                    axis=1,
                )
                for field in range(fields)
            ],
            axis=0,
        )
        coarse = window.astype(jnp.bfloat16)
        fine = (window - coarse.astype(jnp.float32)).astype(jnp.bfloat16)

        def product(values, part):
            return jnp.dot(values, band_ref[part], preferred_element_type=jnp.float32)

        turned = product(fine, 0) + product(coarse, 1) + product(coarse, 0)
        angular = [turned[field * chunk : (field + 1) * chunk] for field in range(fields)]

        def axial(field):
            total = mix_ref[plane * planes] * own_ref[field, 0, lines]
            for other in range(1, planes):
                total = total + mix_ref[plane * planes + other] * own_ref[field, other, lines]
            return total

        def radial(which):
            tall = tall_ref[which, plane, pl.ds(first, chunk + 2 * TILE)]
            total = jnp.zeros((chunk, cells), jnp.float32)
            for reach, weight in enumerate(WEIGHTS, start=1):
                upper = tall[TILE + reach : TILE + reach + chunk]
                lower = tall[TILE - reach : TILE - reach + chunk]
                total = total + weight * (upper - lower)
            return total

        stream, speed_sq, turning, metric = (wide(kind) for kind in range(4))
        deriv_1, deriv_4 = axial(1), axial(4)
        spread = deriv_1 + metric * angular[3] + radial(0)
        out_ref[0, plane, lines] = -(stream * axial(0) + turning * angular[0] + spread)
        out_ref[1, plane, lines] = -(stream * deriv_1 + turning * angular[1] + deriv_4)
        out_ref[2, plane, lines] = -(stream * axial(2) + turning * angular[2] + radial(1))
        out_ref[3, plane, lines] = -(
            stream * axial(3) + turning * angular[3] + metric * angular[4]
        )
        out_ref[4, plane, lines] = -(
            stream * deriv_4 + turning * angular[4] + speed_sq * spread
        )
        return carry

    lax.fori_loop(0, planes * (rows // chunk), body, 0)


def facing_kernel(first_row, part_ref, facing_ref, scale_ref, *refs):
    out_ref, stage_ref, sems = refs[-3:]
    side = lax.axis_index("axl")
    sign = jnp.where(side == 0, 1.0, -1.0).astype(jnp.float32)
    fields, planes, _, cells = part_ref.shape
    rows = facing_ref.shape[2]
    count = rows // TILE

    def copies(step):
        start = pl.multiple_of(step * TILE, TILE)
        return [
            pltpu.make_async_copy(
                stage_ref.at[:, near, pl.ds(start, TILE)],
                out_ref.at[:, near_plane(near, planes), pl.ds(first_row + start, TILE)],
                sems.at[REACH * step + near],
            )
            for near in range(REACH)
        ]

    if first_row == 0:
        far = near_plane(REACH, planes)
        spare = pltpu.make_async_copy(part_ref.at[:, far], out_ref.at[:, far], sems.at[REACH * count])
        spare.start()

    def body(step, carry):
        start = pl.multiple_of(step * TILE, TILE)
        lines, here = pl.ds(first_row + start, TILE), pl.ds(start, TILE)
        for near in range(REACH):
            plane = near_plane(near, planes)

            def wide(kind):
                half = scale_ref[kind, plane, lines]
                return jnp.concatenate([half, half], axis=1)

            def deriv(field):
                total = (sign * WEIGHTS[near]) * facing_ref[field, 0, here]
                for other in range(1, REACH - near):
                    total = total + (sign * WEIGHTS[near + other]) * facing_ref[field, other, here]
                return total

            stream, speed_sq = wide(0), wide(1)
            derivs = [deriv(field) for field in range(fields)]
            extra = [derivs[1], derivs[4], None, None, speed_sq * derivs[1]]
            for field in range(fields):
                change = stream * derivs[field]
                if extra[field] is not None:
                    change = change + extra[field]
                stage_ref[field, near, here] = part_ref[field, plane, lines] - change
        for copy in copies(step):
            copy.start()
        return carry

    def finish(step, carry):
        for copy in copies(step):
            copy.wait()
        return carry

    lax.fori_loop(0, count, body, 0)
    lax.fori_loop(0, count, finish, 0)
    if first_row == 0:
        spare.wait()


def per_device(perturbation, axial_velocity, swirl_velocity, sound_speed, rotor_offset):
    fields, planes, rows, cells = perturbation.shape
    azi_count, rad_count = lax.axis_size("azi"), lax.axis_size("rad")
    blocks = (rotor_offset[0] + BAND) // cells % azi_count

    index = (lax.axis_index("rad") * rows + jnp.arange(rows, dtype=jnp.int32)).astype(jnp.float32)
    metric = 2.0 / (1.0 + (index + 0.5) / (rows * rad_count))

    def spread_scales(axial_velocity, swirl_velocity, sound_speed):
        scales = jnp.stack(
            [
                axial_velocity,
                sound_speed * sound_speed,
                swirl_velocity * metric,
                jnp.broadcast_to(metric, axial_velocity.shape),
            ]
        )
        return jnp.broadcast_to(scales[..., None], scales.shape + (BAND,))

    table = band_table(stencil_coefs(NA, BAND), cells).astype(np.float32)
    coarse = table.astype(ml_dtypes.bfloat16)
    fine = (table - coarse.astype(np.float32)).astype(ml_dtypes.bfloat16)
    band = jnp.asarray(np.stack([coarse, fine]))
    mix = np.zeros((planes, planes))
    for reach, weight in enumerate(WEIGHTS, start=1):
        mix += weight * (np.eye(planes, k=reach) - np.eye(planes, k=-reach))
    mix = jnp.asarray(mix.reshape(-1), dtype=jnp.float32)

    rows_a = ROWS_A
    rows_b = rows - rows_a

    def array(*shape):
        return jax.ShapeDtypeStruct(shape, jnp.float32)

    def exchange(first, second):
        left = lax.ppermute(second, "azi", neighbours("azi", 1, True))
        right = lax.ppermute(first, "azi", neighbours("azi", -1, True))
        return left, right

    def rotate(before, first_row, count, *values):
        return pl.pallas_call(
            lambda *refs: rotate_kernel(before, first_row, *refs),
            out_shape=array(fields, 3, count, cells),
            in_specs=[SMEM, VMEM, VMEM, VMEM],
            out_specs=VMEM,
            compiler_params=PARAMS,
            cost_estimate=FREE,
            name="rotate",
        )(*values)

    def facing_step(first, part, facing, scales, *done):
        return pl.pallas_call(
            lambda *refs: facing_kernel(first, *refs),
            out_shape=array(*part.shape),
            in_specs=[VMEM] * 3 + [HBM] * len(done),
            out_specs=HBM,
            scratch_shapes=[
                pltpu.VMEM(facing.shape, jnp.float32),
                pltpu.SemaphoreType.DMA((REACH * (facing.shape[2] // TILE) + 1,)),
            ],
            input_output_aliases={3: 0} if done else {},
            compiler_params=PARAMS,
            cost_estimate=FREE,
            name="facing",
        )(part, facing, scales, *done)

    def branch(shift):
        pairs = facing_pairs(shift)

        def run(rotor_offset, mix, perturbation, band, *speeds):
            sent_a = pl.pallas_call(
                facing_edge_kernel,
                out_shape=array(fields, 3, rows_a, cells),
                in_specs=[ANY],
                out_specs=VMEM,
                scratch_shapes=[pltpu.SemaphoreType.DMA((3,))],
                compiler_params=PARAMS,
                cost_estimate=FREE,
                name="facing_edge",
            )(perturbation)
            first, second, top, bottom = pl.pallas_call(
                edges_kernel,
                out_shape=(array(fields, planes, rows, BAND),) * 2 + (array(REACH, 2 * planes, cells),) * 2,
                in_specs=[VMEM, ANY],
                out_specs=(VMEM,) * 4,
                scratch_shapes=[pltpu.SemaphoreType.DMA((2,))],
                compiler_params=PARAMS,
                cost_estimate=FREE,
                name="edges",
            )(perturbation, sent_a)
            left, right = exchange(first, second)
            low = lax.ppermute(bottom, "rad", neighbours("rad", 1, False))
            high = lax.ppermute(top, "rad", neighbours("rad", -1, False))
            facing_a = lax.ppermute(sent_a, AXES, pairs)
            left, right, speeds = lax.optimization_barrier((left, right, speeds))
            scales = spread_scales(*speeds)
            sent_b = rotate(True, rows_a, rows_b, rotor_offset, perturbation, left, right)
            facing_b = lax.ppermute(sent_b, AXES, pairs)
            part = pl.pallas_call(
                local_kernel,
                out_shape=array(*perturbation.shape),
                in_specs=[SMEM] + [VMEM] * 7,
                out_specs=VMEM,
                scratch_shapes=[pltpu.VMEM((2, planes, rows + 2 * TILE, cells), jnp.float32)],
                compiler_params=PARAMS,
                cost_estimate=FREE,
                name="local",
            )(mix, perturbation, left, right, low, high, scales, band)
            halves = pl.pallas_call(
                split_kernel,
                out_shape=(array(fields, 3, rows_a, BAND),) * 2,
                in_specs=[ANY],
                out_specs=(VMEM,) * 2,
                scratch_shapes=[pltpu.SemaphoreType.DMA((2,))],
                compiler_params=PARAMS,
                cost_estimate=FREE,
                name="split",
            )(facing_a)
            turned_a = rotate(False, 0, rows_a, rotor_offset, facing_a, *exchange(*halves))
            done_a = facing_step(0, part, turned_a, scales)
            return facing_step(rows_a, part, facing_b, scales, done_a)

        return run

    mix, band = lax.optimization_barrier((mix, band))
    return lax.switch(
        blocks,
        [branch(shift) for shift in range(azi_count)],
        rotor_offset, mix, perturbation, band, axial_velocity, swirl_velocity, sound_speed,
    )


def solution(mesh):
    return jax.shard_map(
        per_device,
        mesh=mesh,
        in_specs=(
            P(None, "axl", "rad", "azi"),
            P("axl", "rad"),
            P("axl", "rad"),
            P("axl", "rad"),
            P(),
        ),
        out_specs=P(None, "axl", "rad", "azi"),
        check_vma=False,
    )
```

```python
import jax
import jax.numpy as jnp
import ml_dtypes
import numpy as np
from jax import lax
from jax.experimental import pallas as pl
from jax.experimental.pallas import tpu as pltpu
from jax.sharding import PartitionSpec as P

NA = 2048
BAND = 128
WEIGHTS = (45.0 / 60.0, -9.0 / 60.0, 1.0 / 60.0)
AXES = ("azi", "rad", "axl")
TILE = 8
VMEM = pl.BlockSpec(memory_space=pltpu.VMEM)
SMEM = pl.BlockSpec(memory_space=pltpu.SMEM)
ANY = pl.BlockSpec(memory_space=pl.ANY)
HBM = pl.BlockSpec(memory_space=pltpu.HBM)
REACH = 3
ROWS_A = 16
FREE = pl.CostEstimate(flops=0, bytes_accessed=0, transcendentals=0)
PARAMS = pltpu.CompilerParams(vmem_limit_bytes=12 * 2**20)


def stencil_coefs(cells, reach):
    offsets = np.arange(1, reach + 1)
    signs = np.where(offsets % 2 == 1, 1.0, -1.0)
    angles = np.pi * offsets / cells
    values = np.pi / cells * signs * np.cos(angles) / np.sin(angles)
    return np.concatenate([np.zeros(1), values])


def band_table(coefs, columns):
    reach = coefs.shape[0] - 1
    source = np.arange(columns + 2 * reach)
    target = np.arange(columns)
    offsets = source[:, None] - target[None, :] - reach
    magnitude = np.abs(offsets)
    picked = coefs[np.minimum(magnitude, reach)]
    return np.where(magnitude <= reach, np.sign(offsets) * picked, 0.0)


def neighbours(axis, step, wrap):
    count = lax.axis_size(axis)
    pairs = [(i, (i + step) % count) for i in range(count)]
    return pairs if wrap else [(i, j) for i, j in pairs if abs(i - j) == 1]


def facing_pairs(blocks):
    azi_count, rad_count = lax.axis_size("azi"), lax.axis_size("rad")

    def place(azi, rad, axl):
        return (azi % azi_count * rad_count + rad) * 2 + axl

    pairs = []
    for azi in range(azi_count):
        for rad in range(rad_count):
            pairs.append((place(azi, rad, 0), place(azi - blocks, rad, 1)))
            pairs.append((place(azi, rad, 1), place(azi + blocks, rad, 0)))
    return pairs


def near_plane(near, planes):
    return jnp.where(lax.axis_index("axl") == 0, planes - 1 - near, near)


def run_copies(pairs, sems):
    copies = [pltpu.make_async_copy(a, b, sems.at[i]) for i, (a, b) in enumerate(pairs)]
    for copy in copies:
        copy.start()
    for copy in copies:
        copy.wait()


def facing_edge_kernel(own_ref, out_ref, sems):
    planes, rows = own_ref.shape[1], out_ref.shape[2]
    run_copies(
        [
            (own_ref.at[:, near_plane(near, planes), pl.ds(TILE, rows)], out_ref.at[:, near])
            for near in range(3)
        ],
        sems,
    )


def edges_kernel(own_ref, _, first_ref, second_ref, top_ref, bottom_ref, sems):
    planes, rows = own_ref.shape[1:3]
    pairs = [
        (own_ref.at[:, :, :, pl.ds(0, BAND)], first_ref),
        (own_ref.at[:, :, :, pl.ds(BAND, BAND)], second_ref),
    ]
    copies = [pltpu.make_async_copy(a, b, sems.at[i]) for i, (a, b) in enumerate(pairs)]
    for copy in copies:
        copy.start()

    def line_of(line, carry):
        field, plane = 2 + 2 * (line // planes), line % planes
        head = own_ref[field, plane, :TILE]
        tail = own_ref[field, plane, rows - TILE :]
        for step in range(REACH):
            top_ref[step, pl.ds(line, 1)] = head[step : step + 1]
            bottom_ref[step, pl.ds(line, 1)] = tail[TILE - REACH + step : TILE - REACH + step + 1]
        return carry

    lax.fori_loop(0, 2 * planes, line_of, 0)
    for copy in copies:
        copy.wait()


def split_kernel(own_ref, first_ref, second_ref, sems):
    run_copies(
        [
            (own_ref.at[:, :, :, pl.ds(0, BAND)], first_ref),
            (own_ref.at[:, :, :, pl.ds(BAND, BAND)], second_ref),
        ],
        sems,
    )


def rotate_kernel(before, runs, offset_ref, own_ref, left_ref, right_ref, out_ref):
    fields, _, rows, cells = out_ref.shape
    moved = (offset_ref[0] + BAND) % cells
    forward = lax.axis_index("axl") == (0 if before else 1)
    start = jnp.where(forward, moved, cells - moved)
    tile, turn = start // BAND, start % BAND
    back = (BAND - turn) % BAND

    def take(ref, field, plane, *cells):
        return jnp.concatenate([ref[(field, plane, pl.ds(*run), *cells)] for run in runs], axis=0)

    def body(field, carry):
        keep = lax.broadcasted_iota(jnp.int32, (rows, BAND), 1) < BAND - turn
        for near in range(3):
            plane = near_plane(near, own_ref.shape[1]) if before else near
            tiles = [
                take(left_ref, field, plane),
                take(own_ref, field, plane, slice(0, BAND)),
                take(own_ref, field, plane, slice(BAND, 2 * BAND)),
                take(right_ref, field, plane),
            ]
            tiles.append(tiles[-1])
            turned = [
                pltpu.roll(
                    jnp.where(tile == 0, tiles[i], jnp.where(tile == 1, tiles[i + 1], tiles[i + 2])),
                    back,
                    1,
                )
                for i in range(3)
            ]
            out_ref[field, near, :, :BAND] = jnp.where(keep, turned[0], turned[1])
            out_ref[field, near, :, BAND:] = jnp.where(keep, turned[1], turned[2])
        return carry

    lax.fori_loop(0, fields, body, 0)


def local_kernel(
    mix_ref, own_ref, left_ref, right_ref, scale_ref, band_ref, out_ref, tall_ref
):
    fields, planes, rows, cells = own_ref.shape
    chunk = 2 * TILE

    def fill(line, carry):
        which, plane = line // planes, line % planes
        blank = jnp.zeros((TILE, cells), jnp.float32)
        tall_ref[which, plane, :TILE] = blank
        tall_ref[which, plane, TILE : TILE + rows] = own_ref[2 + 2 * which, plane]
        tall_ref[which, plane, TILE + rows :] = blank
        return carry

    lax.fori_loop(0, 2 * planes, fill, 0)

    def body(step, carry):
        plane, place = step % planes, step // planes
        first = pl.multiple_of(place * chunk, chunk)
        lines = pl.ds(first, chunk)

        def wide(kind):
            half = scale_ref[kind, plane, lines]
            return jnp.concatenate([half, half], axis=1)

        window = jnp.concatenate(
            [
                jnp.concatenate(
                    [
                        left_ref[field, plane, lines],
                        own_ref[field, plane, lines],
                        right_ref[field, plane, lines],
                    ],
                    axis=1,
                )
                for field in range(fields)
            ],
            axis=0,
        )
        coarse = window.astype(jnp.bfloat16)
        fine = (window - coarse.astype(jnp.float32)).astype(jnp.bfloat16)

        def product(values, part):
            return jnp.dot(values, band_ref[part], preferred_element_type=jnp.float32)

        turned = product(fine, 0) + product(coarse, 1) + product(coarse, 0)
        angular = [turned[field * chunk : (field + 1) * chunk] for field in range(fields)]

        def axial(field):
            total = mix_ref[plane * planes] * own_ref[field, 0, lines]
            for other in range(1, planes):
                total = total + mix_ref[plane * planes + other] * own_ref[field, other, lines]
            return total

        def radial(which):
            tall = tall_ref[which, plane, pl.ds(first, chunk + 2 * TILE)]
            total = jnp.zeros((chunk, cells), jnp.float32)
            for reach, weight in enumerate(WEIGHTS, start=1):
                upper = tall[TILE + reach : TILE + reach + chunk]
                lower = tall[TILE - reach : TILE - reach + chunk]
                total = total + weight * (upper - lower)
            return total

        stream, speed_sq, turning, metric = (wide(kind) for kind in range(4))
        deriv_1, deriv_4 = axial(1), axial(4)
        spread = deriv_1 + metric * angular[3] + radial(0)
        out_ref[0, plane, lines] = -(stream * axial(0) + turning * angular[0] + spread)
        out_ref[1, plane, lines] = -(stream * deriv_1 + turning * angular[1] + deriv_4)
        out_ref[2, plane, lines] = -(stream * axial(2) + turning * angular[2] + radial(1))
        out_ref[3, plane, lines] = -(
            stream * axial(3) + turning * angular[3] + metric * angular[4]
        )
        out_ref[4, plane, lines] = -(
            stream * deriv_4 + turning * angular[4] + speed_sq * spread
        )
        return carry

    lax.fori_loop(0, planes * (rows // chunk), body, 0)


def facing_kernel(inner, part_ref, facing_ref, scale_ref, *refs):
    out_ref, stage_ref, sems = refs[-3:]
    side = lax.axis_index("axl")
    sign = jnp.where(side == 0, 1.0, -1.0).astype(jnp.float32)
    fields, planes, all_rows, cells = part_ref.shape
    rows = facing_ref.shape[2]
    count = rows // TILE

    def row_of(step):
        tile = step + 1 if inner else jnp.where(step == 0, 0, step + (all_rows - rows) // TILE)
        return pl.multiple_of(tile * TILE, TILE)

    def copies(step):
        return [
            pltpu.make_async_copy(
                stage_ref.at[:, near, pl.ds(pl.multiple_of(step * TILE, TILE), TILE)],
                out_ref.at[:, near_plane(near, planes), pl.ds(row_of(step), TILE)],
                sems.at[planes * step + near],
            )
            for near in range(planes)
        ]

    def radial(step, halo_ref, upward):
        def add(near, carry):
            plane = near_plane(near, planes)
            for place in range(REACH):
                row = TILE - 1 - place if upward else place

                def term(which):
                    total = jnp.zeros((1, cells), jnp.float32)
                    for other in range(place, REACH):
                        weight = WEIGHTS[place + REACH - 1 - other]
                        source = REACH - 1 - other if upward else other
                        value = halo_ref[source, pl.ds(which * planes + plane, 1)]
                        total = total + (weight if upward else -weight) * value
                    return total

                half = scale_ref[1, plane, pl.ds(row_of(step) + row, 1)]
                speed_sq = jnp.concatenate([half, half], axis=1)
                first, second = term(0), term(1)
                here = pl.ds(step * TILE + row, 1)
                stage_ref[0, near, here] = stage_ref[0, near, here] - first
                stage_ref[2, near, here] = stage_ref[2, near, here] - second
                stage_ref[4, near, here] = stage_ref[4, near, here] - speed_sq * first
            return carry

        lax.fori_loop(0, planes, add, 0)

    def body(step, carry):
        start = pl.multiple_of(step * TILE, TILE)
        lines, here = pl.ds(row_of(step), TILE), pl.ds(start, TILE)
        for field in range(fields):
            stage_ref[field, REACH, here] = part_ref[field, near_plane(REACH, planes), lines]
        for near in range(REACH):
            plane = near_plane(near, planes)

            def wide(kind):
                half = scale_ref[kind, plane, lines]
                return jnp.concatenate([half, half], axis=1)

            def deriv(field):
                total = (sign * WEIGHTS[near]) * facing_ref[field, 0, here]
                for other in range(1, REACH - near):
                    total = total + (sign * WEIGHTS[near + other]) * facing_ref[field, other, here]
                return total

            stream, speed_sq = wide(0), wide(1)
            derivs = [deriv(field) for field in range(fields)]
            extra = [derivs[1], derivs[4], None, None, speed_sq * derivs[1]]
            for field in range(fields):
                change = stream * derivs[field]
                if extra[field] is not None:
                    change = change + extra[field]
                stage_ref[field, near, here] = part_ref[field, plane, lines] - change
        if not inner:
            pl.when(step == 0)(lambda: radial(0, refs[0], False))
            pl.when(step == count - 1)(lambda: radial(count - 1, refs[1], True))
        for copy in copies(step):
            copy.start()
        return carry

    def finish(step, carry):
        for copy in copies(step):
            copy.wait()
        return carry

    lax.fori_loop(0, count, body, 0)
    lax.fori_loop(0, count, finish, 0)


def per_device(perturbation, axial_velocity, swirl_velocity, sound_speed, rotor_offset):
    fields, planes, rows, cells = perturbation.shape
    azi_count, rad_count = lax.axis_size("azi"), lax.axis_size("rad")
    blocks = (rotor_offset[0] + BAND) // cells % azi_count

    index = (lax.axis_index("rad") * rows + jnp.arange(rows, dtype=jnp.int32)).astype(jnp.float32)
    metric = 2.0 / (1.0 + (index + 0.5) / (rows * rad_count))

    def spread_scales(axial_velocity, swirl_velocity, sound_speed):
        scales = jnp.stack(
            [
                axial_velocity,
                sound_speed * sound_speed,
                swirl_velocity * metric,
                jnp.broadcast_to(metric, axial_velocity.shape),
            ]
        )
        return jnp.broadcast_to(scales[..., None], scales.shape + (BAND,))

    table = band_table(stencil_coefs(NA, BAND), cells).astype(np.float32)
    coarse = table.astype(ml_dtypes.bfloat16)
    fine = (table - coarse.astype(np.float32)).astype(ml_dtypes.bfloat16)
    band = jnp.asarray(np.stack([coarse, fine]))
    mix = np.zeros((planes, planes))
    for reach, weight in enumerate(WEIGHTS, start=1):
        mix += weight * (np.eye(planes, k=reach) - np.eye(planes, k=-reach))
    mix = jnp.asarray(mix.reshape(-1), dtype=jnp.float32)

    rows_a = ROWS_A

    def array(*shape):
        return jax.ShapeDtypeStruct(shape, jnp.float32)

    def exchange(first, second):
        left = lax.ppermute(second, "azi", neighbours("azi", 1, True))
        right = lax.ppermute(first, "azi", neighbours("azi", -1, True))
        return left, right

    def rotate(before, runs, *values):
        count = sum(run[1] for run in runs)
        return pl.pallas_call(
            lambda *refs: rotate_kernel(before, runs, *refs),
            out_shape=array(fields, 3, count, cells),
            in_specs=[SMEM, VMEM, VMEM, VMEM],
            out_specs=VMEM,
            compiler_params=PARAMS,
            cost_estimate=FREE,
            name="rotate",
        )(*values)

    def facing_step(part, facing, scales, *rest):
        fields, _, count, cells = facing.shape
        return pl.pallas_call(
            lambda *refs: facing_kernel(not rest, *refs),
            out_shape=array(*part.shape),
            in_specs=[VMEM] * 3 + [VMEM, VMEM, HBM][: len(rest)],
            out_specs=HBM,
            scratch_shapes=[
                pltpu.VMEM((fields, planes, count, cells), jnp.float32),
                pltpu.SemaphoreType.DMA((planes * (count // TILE),)),
            ],
            input_output_aliases={5: 0} if rest else {},
            compiler_params=PARAMS,
            cost_estimate=FREE,
            name="facing",
        )(part, facing, scales, *rest)

    def branch(shift):
        pairs = facing_pairs(shift)

        def run(rotor_offset, mix, perturbation, band, *speeds):
            sent_a = pl.pallas_call(
                facing_edge_kernel,
                out_shape=array(fields, 3, rows_a, cells),
                in_specs=[ANY],
                out_specs=VMEM,
                scratch_shapes=[pltpu.SemaphoreType.DMA((3,))],
                compiler_params=PARAMS,
                cost_estimate=FREE,
                name="facing_edge",
            )(perturbation)
            first, second, top, bottom = pl.pallas_call(
                edges_kernel,
                out_shape=(array(fields, planes, rows, BAND),) * 2 + (array(REACH, 2 * planes, cells),) * 2,
                in_specs=[VMEM, ANY],
                out_specs=(VMEM,) * 4,
                scratch_shapes=[pltpu.SemaphoreType.DMA((2,))],
                compiler_params=PARAMS,
                cost_estimate=FREE,
                name="edges",
            )(perturbation, sent_a)
            left, right = exchange(first, second)
            low = lax.ppermute(bottom, "rad", neighbours("rad", 1, False))
            high = lax.ppermute(top, "rad", neighbours("rad", -1, False))
            facing_a = lax.ppermute(sent_a, AXES, pairs)
            left, right, speeds = lax.optimization_barrier((left, right, speeds))
            scales = spread_scales(*speeds)
            sent_b = rotate(True, [(0, TILE), (TILE + rows_a, rows - TILE - rows_a)], rotor_offset, perturbation, left, right)
            facing_b = lax.ppermute(sent_b, AXES, pairs)
            part = pl.pallas_call(
                local_kernel,
                out_shape=array(*perturbation.shape),
                in_specs=[SMEM] + [VMEM] * 5,
                out_specs=VMEM,
                scratch_shapes=[pltpu.VMEM((2, planes, rows + 2 * TILE, cells), jnp.float32)],
                compiler_params=PARAMS,
                cost_estimate=FREE,
                name="local",
            )(mix, perturbation, left, right, scales, band)
            halves = pl.pallas_call(
                split_kernel,
                out_shape=(array(fields, 3, rows_a, BAND),) * 2,
                in_specs=[ANY],
                out_specs=(VMEM,) * 2,
                scratch_shapes=[pltpu.SemaphoreType.DMA((2,))],
                compiler_params=PARAMS,
                cost_estimate=FREE,
                name="split",
            )(facing_a)
            turned_a = rotate(False, [(0, rows_a)], rotor_offset, facing_a, *exchange(*halves))
            done_a = facing_step(part, turned_a, scales)
            return facing_step(part, facing_b, scales, low, high, done_a)

        return run

    mix, band = lax.optimization_barrier((mix, band))
    return lax.switch(
        blocks,
        [branch(shift) for shift in range(azi_count)],
        rotor_offset, mix, perturbation, band, axial_velocity, swirl_velocity, sound_speed,
    )


def solution(mesh):
    return jax.shard_map(
        per_device,
        mesh=mesh,
        in_specs=(
            P(None, "axl", "rad", "azi"),
            P("axl", "rad"),
            P("axl", "rad"),
            P("axl", "rad"),
            P(),
        ),
        out_specs=P(None, "axl", "rad", "azi"),
        check_vma=False,
    )
```

```python
import jax
import jax.numpy as jnp
import ml_dtypes
import numpy as np
from jax import lax
from jax.experimental import pallas as pl
from jax.experimental.pallas import tpu as pltpu
from jax.sharding import PartitionSpec as P

NA = 2048
BAND = 128
WEIGHTS = (45.0 / 60.0, -9.0 / 60.0, 1.0 / 60.0)
AXES = ("azi", "rad", "axl")
TILE = 8
VMEM = pl.BlockSpec(memory_space=pltpu.VMEM)
SMEM = pl.BlockSpec(memory_space=pltpu.SMEM)
ANY = pl.BlockSpec(memory_space=pl.ANY)
HBM = pl.BlockSpec(memory_space=pltpu.HBM)
REACH = 3
ROWS_A = 32
FREE = pl.CostEstimate(flops=0, bytes_accessed=0, transcendentals=0)
PARAMS = pltpu.CompilerParams(vmem_limit_bytes=12 * 2**20)


def stencil_coefs(cells, reach):
    offsets = np.arange(1, reach + 1)
    signs = np.where(offsets % 2 == 1, 1.0, -1.0)
    angles = np.pi * offsets / cells
    values = np.pi / cells * signs * np.cos(angles) / np.sin(angles)
    return np.concatenate([np.zeros(1), values])


def band_table(coefs, columns):
    reach = coefs.shape[0] - 1
    source = np.arange(columns + 2 * reach)
    target = np.arange(columns)
    offsets = source[:, None] - target[None, :] - reach
    magnitude = np.abs(offsets)
    picked = coefs[np.minimum(magnitude, reach)]
    return np.where(magnitude <= reach, np.sign(offsets) * picked, 0.0)


def neighbours(axis, step, wrap):
    count = lax.axis_size(axis)
    pairs = [(i, (i + step) % count) for i in range(count)]
    return pairs if wrap else [(i, j) for i, j in pairs if abs(i - j) == 1]


def facing_pairs(blocks):
    azi_count, rad_count = lax.axis_size("azi"), lax.axis_size("rad")

    def place(azi, rad, axl):
        return (azi % azi_count * rad_count + rad) * 2 + axl

    pairs = []
    for azi in range(azi_count):
        for rad in range(rad_count):
            pairs.append((place(azi, rad, 0), place(azi - blocks, rad, 1)))
            pairs.append((place(azi, rad, 1), place(azi + blocks, rad, 0)))
    return pairs


def near_plane(near, planes):
    return jnp.where(lax.axis_index("axl") == 0, planes - 1 - near, near)


def run_copies(pairs, sems):
    copies = [pltpu.make_async_copy(a, b, sems.at[i]) for i, (a, b) in enumerate(pairs)]
    for copy in copies:
        copy.start()
    for copy in copies:
        copy.wait()


def facing_edge_kernel(own_ref, out_ref, sems):
    planes, rows = own_ref.shape[1], out_ref.shape[2]
    run_copies(
        [
            (own_ref.at[:, near_plane(near, planes), pl.ds(TILE, rows)], out_ref.at[:, near])
            for near in range(3)
        ],
        sems,
    )


def edges_kernel(own_ref, _, first_ref, second_ref, top_ref, bottom_ref, sems):
    planes, rows = own_ref.shape[1:3]
    pairs = [
        (own_ref.at[:, :, :, pl.ds(0, BAND)], first_ref),
        (own_ref.at[:, :, :, pl.ds(BAND, BAND)], second_ref),
    ]
    copies = [pltpu.make_async_copy(a, b, sems.at[i]) for i, (a, b) in enumerate(pairs)]
    for copy in copies:
        copy.start()

    def line_of(line, carry):
        field, plane = 2 + 2 * (line // planes), line % planes
        head = own_ref[field, plane, :TILE]
        tail = own_ref[field, plane, rows - TILE :]
        for step in range(REACH):
            top_ref[step, pl.ds(line, 1)] = head[step : step + 1]
            bottom_ref[step, pl.ds(line, 1)] = tail[TILE - REACH + step : TILE - REACH + step + 1]
        return carry

    lax.fori_loop(0, 2 * planes, line_of, 0)
    for copy in copies:
        copy.wait()


def split_kernel(own_ref, first_ref, second_ref, sems):
    run_copies(
        [
            (own_ref.at[:, :, :, pl.ds(0, BAND)], first_ref),
            (own_ref.at[:, :, :, pl.ds(BAND, BAND)], second_ref),
        ],
        sems,
    )


def rotate_kernel(before, runs, offset_ref, own_ref, left_ref, right_ref, out_ref):
    fields, _, rows, cells = out_ref.shape
    moved = (offset_ref[0] + BAND) % cells
    forward = lax.axis_index("axl") == (0 if before else 1)
    start = jnp.where(forward, moved, cells - moved)
    tile, turn = start // BAND, start % BAND
    back = (BAND - turn) % BAND

    def take(ref, field, plane, *cells):
        return jnp.concatenate([ref[(field, plane, pl.ds(*run), *cells)] for run in runs], axis=0)

    def body(field, carry):
        keep = lax.broadcasted_iota(jnp.int32, (rows, BAND), 1) < BAND - turn
        for near in range(3):
            plane = near_plane(near, own_ref.shape[1]) if before else near
            tiles = [
                take(left_ref, field, plane),
                take(own_ref, field, plane, slice(0, BAND)),
                take(own_ref, field, plane, slice(BAND, 2 * BAND)),
                take(right_ref, field, plane),
            ]
            tiles.append(tiles[-1])
            turned = [
                pltpu.roll(
                    jnp.where(tile == 0, tiles[i], jnp.where(tile == 1, tiles[i + 1], tiles[i + 2])),
                    back,
                    1,
                )
                for i in range(3)
            ]
            out_ref[field, near, :, :BAND] = jnp.where(keep, turned[0], turned[1])
            out_ref[field, near, :, BAND:] = jnp.where(keep, turned[1], turned[2])
        return carry

    lax.fori_loop(0, fields, body, 0)


def local_kernel(
    mix_ref, own_ref, left_ref, right_ref, scale_ref, band_ref, out_ref, tall_ref
):
    fields, planes, rows, cells = own_ref.shape
    chunk = 2 * TILE

    def fill(line, carry):
        which, plane = line // planes, line % planes
        blank = jnp.zeros((TILE, cells), jnp.float32)
        tall_ref[which, plane, :TILE] = blank
        tall_ref[which, plane, TILE : TILE + rows] = own_ref[2 + 2 * which, plane]
        tall_ref[which, plane, TILE + rows :] = blank
        return carry

    lax.fori_loop(0, 2 * planes, fill, 0)

    def body(step, carry):
        plane, place = step % planes, step // planes
        first = pl.multiple_of(place * chunk, chunk)
        lines = pl.ds(first, chunk)

        def wide(kind):
            half = scale_ref[kind, plane, lines]
            return jnp.concatenate([half, half], axis=1)

        window = jnp.concatenate(
            [
                jnp.concatenate(
                    [
                        left_ref[field, plane, lines],
                        own_ref[field, plane, lines],
                        right_ref[field, plane, lines],
                    ],
                    axis=1,
                )
                for field in range(fields)
            ],
            axis=0,
        )
        coarse = window.astype(jnp.bfloat16)
        fine = (window - coarse.astype(jnp.float32)).astype(jnp.bfloat16)

        def product(values, part):
            return jnp.dot(values, band_ref[part], preferred_element_type=jnp.float32)

        turned = product(fine, 0) + product(coarse, 1) + product(coarse, 0)
        angular = [turned[field * chunk : (field + 1) * chunk] for field in range(fields)]

        def axial(field):
            total = mix_ref[plane * planes] * own_ref[field, 0, lines]
            for other in range(1, planes):
                total = total + mix_ref[plane * planes + other] * own_ref[field, other, lines]
            return total

        def radial(which):
            tall = tall_ref[which, plane, pl.ds(first, chunk + 2 * TILE)]
            total = jnp.zeros((chunk, cells), jnp.float32)
            for reach, weight in enumerate(WEIGHTS, start=1):
                upper = tall[TILE + reach : TILE + reach + chunk]
                lower = tall[TILE - reach : TILE - reach + chunk]
                total = total + weight * (upper - lower)
            return total

        stream, speed_sq, turning, metric = (wide(kind) for kind in range(4))
        deriv_1, deriv_4 = axial(1), axial(4)
        spread = deriv_1 + metric * angular[3] + radial(0)
        out_ref[0, plane, lines] = -(stream * axial(0) + turning * angular[0] + spread)
        out_ref[1, plane, lines] = -(stream * deriv_1 + turning * angular[1] + deriv_4)
        out_ref[2, plane, lines] = -(stream * axial(2) + turning * angular[2] + radial(1))
        out_ref[3, plane, lines] = -(
            stream * axial(3) + turning * angular[3] + metric * angular[4]
        )
        out_ref[4, plane, lines] = -(
            stream * deriv_4 + turning * angular[4] + speed_sq * spread
        )
        return carry

    lax.fori_loop(0, planes * (rows // chunk), body, 0)


def facing_kernel(inner, part_ref, facing_ref, scale_ref, *refs):
    out_ref, stage_ref, sems = refs[-3:]
    side = lax.axis_index("axl")
    sign = jnp.where(side == 0, 1.0, -1.0).astype(jnp.float32)
    fields, planes, all_rows, cells = part_ref.shape
    rows = facing_ref.shape[2]
    count = rows // TILE

    def row_of(step):
        tile = step + 1 if inner else jnp.where(step == 0, 0, step + (all_rows - rows) // TILE)
        return pl.multiple_of(tile * TILE, TILE)

    def copies(step):
        return [
            pltpu.make_async_copy(
                stage_ref.at[:, near, pl.ds(pl.multiple_of(step * TILE, TILE), TILE)],
                out_ref.at[:, near_plane(near, planes), pl.ds(row_of(step), TILE)],
                sems.at[planes * step + near],
            )
            for near in range(planes)
        ]

    def radial(step, halo_ref, upward):
        def add(near, carry):
            plane = near_plane(near, planes)
            for place in range(REACH):
                row = TILE - 1 - place if upward else place

                def term(which):
                    total = jnp.zeros((1, cells), jnp.float32)
                    for other in range(place, REACH):
                        weight = WEIGHTS[place + REACH - 1 - other]
                        source = REACH - 1 - other if upward else other
                        value = halo_ref[source, pl.ds(which * planes + plane, 1)]
                        total = total + (weight if upward else -weight) * value
                    return total

                half = scale_ref[1, plane, pl.ds(row_of(step) + row, 1)]
                speed_sq = jnp.concatenate([half, half], axis=1)
                first, second = term(0), term(1)
                here = pl.ds(step * TILE + row, 1)
                stage_ref[0, near, here] = stage_ref[0, near, here] - first
                stage_ref[2, near, here] = stage_ref[2, near, here] - second
                stage_ref[4, near, here] = stage_ref[4, near, here] - speed_sq * first
            return carry

        lax.fori_loop(0, planes, add, 0)

    def body(step, carry):
        start = pl.multiple_of(step * TILE, TILE)
        lines, here = pl.ds(row_of(step), TILE), pl.ds(start, TILE)
        for field in range(fields):
            stage_ref[field, REACH, here] = part_ref[field, near_plane(REACH, planes), lines]
        for near in range(REACH):
            plane = near_plane(near, planes)

            def wide(kind):
                half = scale_ref[kind, plane, lines]
                return jnp.concatenate([half, half], axis=1)

            def deriv(field):
                total = (sign * WEIGHTS[near]) * facing_ref[field, 0, here]
                for other in range(1, REACH - near):
                    total = total + (sign * WEIGHTS[near + other]) * facing_ref[field, other, here]
                return total

            stream, speed_sq = wide(0), wide(1)
            derivs = [deriv(field) for field in range(fields)]
            extra = [derivs[1], derivs[4], None, None, speed_sq * derivs[1]]
            for field in range(fields):
                change = stream * derivs[field]
                if extra[field] is not None:
                    change = change + extra[field]
                stage_ref[field, near, here] = part_ref[field, plane, lines] - change
        if not inner:
            pl.when(step == 0)(lambda: radial(0, refs[0], False))
            pl.when(step == count - 1)(lambda: radial(count - 1, refs[1], True))
        for copy in copies(step):
            copy.start()
        return carry

    def finish(step, carry):
        for copy in copies(step):
            copy.wait()
        return carry

    lax.fori_loop(0, count, body, 0)
    lax.fori_loop(0, count, finish, 0)


def per_device(perturbation, axial_velocity, swirl_velocity, sound_speed, rotor_offset):
    fields, planes, rows, cells = perturbation.shape
    azi_count, rad_count = lax.axis_size("azi"), lax.axis_size("rad")
    blocks = (rotor_offset[0] + BAND) // cells % azi_count

    index = (lax.axis_index("rad") * rows + jnp.arange(rows, dtype=jnp.int32)).astype(jnp.float32)
    metric = 2.0 / (1.0 + (index + 0.5) / (rows * rad_count))

    def spread_scales(axial_velocity, swirl_velocity, sound_speed):
        scales = jnp.stack(
            [
                axial_velocity,
                sound_speed * sound_speed,
                swirl_velocity * metric,
                jnp.broadcast_to(metric, axial_velocity.shape),
            ]
        )
        return jnp.broadcast_to(scales[..., None], scales.shape + (BAND,))

    table = band_table(stencil_coefs(NA, BAND), cells).astype(np.float32)
    coarse = table.astype(ml_dtypes.bfloat16)
    fine = (table - coarse.astype(np.float32)).astype(ml_dtypes.bfloat16)
    band = jnp.asarray(np.stack([coarse, fine]))
    mix = np.zeros((planes, planes))
    for reach, weight in enumerate(WEIGHTS, start=1):
        mix += weight * (np.eye(planes, k=reach) - np.eye(planes, k=-reach))
    mix = jnp.asarray(mix.reshape(-1), dtype=jnp.float32)


    def array(*shape):
        return jax.ShapeDtypeStruct(shape, jnp.float32)

    def exchange(first, second):
        left = lax.ppermute(second, "azi", neighbours("azi", 1, True))
        right = lax.ppermute(first, "azi", neighbours("azi", -1, True))
        return left, right

    def rotate(before, runs, *values):
        count = sum(run[1] for run in runs)
        return pl.pallas_call(
            lambda *refs: rotate_kernel(before, runs, *refs),
            out_shape=array(fields, 3, count, cells),
            in_specs=[SMEM, VMEM, VMEM, VMEM],
            out_specs=VMEM,
            compiler_params=PARAMS,
            cost_estimate=FREE,
            name="rotate",
        )(*values)

    def facing_step(part, facing, scales, *rest):
        fields, _, count, cells = facing.shape
        return pl.pallas_call(
            lambda *refs: facing_kernel(not rest, *refs),
            out_shape=array(*part.shape),
            in_specs=[VMEM] * 3 + [VMEM, VMEM, HBM][: len(rest)],
            out_specs=HBM,
            scratch_shapes=[
                pltpu.VMEM((fields, planes, count, cells), jnp.float32),
                pltpu.SemaphoreType.DMA((planes * (count // TILE),)),
            ],
            input_output_aliases={5: 0} if rest else {},
            compiler_params=PARAMS,
            cost_estimate=FREE,
            name="facing",
        )(part, facing, scales, *rest)

    def branch(shift):
        pairs = facing_pairs(shift)
        rows_a = ROWS_A // 2 if 2 * shift == azi_count else ROWS_A

        def run(rotor_offset, mix, perturbation, band, *speeds):
            sent_a = pl.pallas_call(
                facing_edge_kernel,
                out_shape=array(fields, 3, rows_a, cells),
                in_specs=[ANY],
                out_specs=VMEM,
                scratch_shapes=[pltpu.SemaphoreType.DMA((3,))],
                compiler_params=PARAMS,
                cost_estimate=FREE,
                name="facing_edge",
            )(perturbation)
            first, second, top, bottom = pl.pallas_call(
                edges_kernel,
                out_shape=(array(fields, planes, rows, BAND),) * 2 + (array(REACH, 2 * planes, cells),) * 2,
                in_specs=[VMEM, ANY],
                out_specs=(VMEM,) * 4,
                scratch_shapes=[pltpu.SemaphoreType.DMA((2,))],
                compiler_params=PARAMS,
                cost_estimate=FREE,
                name="edges",
            )(perturbation, sent_a)
            left, right = exchange(first, second)
            low = lax.ppermute(bottom, "rad", neighbours("rad", 1, False))
            high = lax.ppermute(top, "rad", neighbours("rad", -1, False))
            facing_a = lax.ppermute(sent_a, AXES, pairs)
            left, right, speeds = lax.optimization_barrier((left, right, speeds))
            scales = spread_scales(*speeds)
            sent_b = rotate(True, [(0, TILE), (TILE + rows_a, rows - TILE - rows_a)], rotor_offset, perturbation, left, right)
            facing_b = lax.ppermute(sent_b, AXES, pairs)
            part = pl.pallas_call(
                local_kernel,
                out_shape=array(*perturbation.shape),
                in_specs=[SMEM] + [VMEM] * 5,
                out_specs=VMEM,
                scratch_shapes=[pltpu.VMEM((2, planes, rows + 2 * TILE, cells), jnp.float32)],
                compiler_params=PARAMS,
                cost_estimate=FREE,
                name="local",
            )(mix, perturbation, left, right, scales, band)
            halves = pl.pallas_call(
                split_kernel,
                out_shape=(array(fields, 3, rows_a, BAND),) * 2,
                in_specs=[ANY],
                out_specs=(VMEM,) * 2,
                scratch_shapes=[pltpu.SemaphoreType.DMA((2,))],
                compiler_params=PARAMS,
                cost_estimate=FREE,
                name="split",
            )(facing_a)
            turned_a = rotate(False, [(0, rows_a)], rotor_offset, facing_a, *exchange(*halves))
            done_a = facing_step(part, turned_a, scales)
            return facing_step(part, facing_b, scales, low, high, done_a)

        return run

    mix, band = lax.optimization_barrier((mix, band))
    return lax.switch(
        blocks,
        [branch(shift) for shift in range(azi_count)],
        rotor_offset, mix, perturbation, band, axial_velocity, swirl_velocity, sound_speed,
    )


def solution(mesh):
    return jax.shard_map(
        per_device,
        mesh=mesh,
        in_specs=(
            P(None, "axl", "rad", "azi"),
            P("axl", "rad"),
            P("axl", "rad"),
            P("axl", "rad"),
            P(),
        ),
        out_specs=P(None, "axl", "rad", "azi"),
        check_vma=False,
    )
```
